128 devices in a mesh: user: 8 (over y, core), item: 16 (over x, z).
Axes of the slice: x: 4, y: 4, z: 4, core: 2. Of those that a mesh axis runs over, the one named last changes fastest.
Arguments:
- weights: bfloat16 [256, 192, 128, 128], P('user', 'item'), may hold values from 0.5 to 8
- ratings: bfloat16 [256, 192, 128, 128], P('user', 'item'), may hold values from -6 to 6
- tile_cols: int32 [256, 192], P('user', 'item'), may hold values from 0 to 31, as said below
- item_factors: bfloat16 [65536, 128], P('item'), may hold values from -1 to 1
- old_users: float32 [32768, 128], P('user'), may hold values from -6 to 6
Outputs:
- new_users: float32 [32768, 128], P(('user', 'item'))
The draws below stay inside these ranges and needn't reach their ends.
Inputs may be any that keep to these rules, and one draw needn't show every extreme that they name: `tile_cols`: within each row, the 12 entries of one item block name distinct tile columns of that block.
All inputs are finite; a program needn't handle non-finite values.
Results may differ from the reference program's by a relative error of at most 0.0065.
Values may be sent and summed in bfloat16 or wider, within the bound.
A program may use at most 128 MiB of HBM per device.

```python
import math
import jax
import jax.numpy as jnp
from jax import lax

K = 128
TILE = 128
SLOTS = 12
ITERS = 3
USERS = 32768
ITEMS = 65536
COL_TILES = 32
TILE_ROWS = 256
TILE_SLOTS = 192
DEVS = 128
PIECE = 2
N_ITEM = 16


def draw_tile_cols(key, part):
    key = jax.random.fold_in(key, 5)
    groups = TILE_ROWS * N_ITEM
    raw = jax.random.randint(key, (groups, COL_TILES), 0, 2 ** 20)
    distinct = raw * COL_TILES + jnp.arange(COL_TILES, dtype=jnp.int32)[None, :]
    order = jnp.argsort(distinct, axis=1, stable=True)[:, :SLOTS]
    return order.reshape(TILE_ROWS, N_ITEM * SLOTS).astype(jnp.int32)


def draw_item_factors(key, part):
    key = jax.random.fold_in(key, 7)
    first, second = jax.random.split(key, 2)
    column_scale = jnp.exp(jax.random.uniform(first, (K,), jnp.float32, math.log(0.22), math.log(2.24)))
    count = float(N_ITEM * SLOTS * TILE)
    base = jnp.clip(jax.random.normal(second, (ITEMS, K), jnp.float32), -6.0, 6.0)
    return (base * column_scale[None, :] / math.sqrt(count)).astype(jnp.bfloat16)


def block_levels(rng, shape, cuts, smallest, top_value):
    def one(position, blocks):
        heights = jax.random.uniform(jax.random.fold_in(jax.random.fold_in(rng, 6), position), (blocks,), jnp.float32, smallest / len(cuts), top_value / len(cuts))
        return jnp.repeat(jnp.exp(heights), shape[position] // blocks).reshape((-1,) + (1,) * (len(shape) - position - 1))

    factor_of = one(*cuts[0])
    for cut in cuts[1:]:
        factor_of = factor_of * one(*cut)
    return factor_of


def normal_values(own_key, shape, width, limit, pieces=(), held_as=jnp.bfloat16):
    drawn = jax.random.normal(own_key, shape, jnp.float32) * width
    if len(pieces) > 0:
        drawn = block_levels(own_key, shape, pieces, -0.22, 0.18) * drawn
    return jnp.clip(drawn, min=-limit, max=limit).astype(held_as)


def setup_inputs(seed: int = 0) -> dict:
    key_list = jax.random.split(jax.random.key(seed), 6)
    weights = jnp.clip(jnp.exp(math.log(8.0) - 2.7725887 * jax.random.uniform(key_list[0], (TILE_ROWS, TILE_SLOTS, TILE, TILE), jnp.float32) ** block_levels(key_list[0], (TILE_ROWS, TILE_SLOTS, TILE, TILE), ((0, 8), (1, 16)), -0.2, 0.2)), 0.5, 8.0).astype(jnp.bfloat16)
    ratings = normal_values(key_list[1], (TILE_ROWS, TILE_SLOTS, TILE, TILE), 1.0, 6.0, ((0, 8), (1, 16)))
    tile_cols = draw_tile_cols(jax.random.fold_in(key_list[5], 71), 0)
    item_factors = draw_item_factors(jax.random.fold_in(key_list[5], 71), 0)
    old_users = normal_values(key_list[4], (USERS, K), 1.0, 6.0, ((0, 8),), jnp.float32)
    return {"weights": weights, "ratings": ratings, "tile_cols": tile_cols, "item_factors": item_factors, "old_users": old_users}


ridge = 0.05


def row_pass(table, weights, ratings, tile_cols, vector, with_ratings):
    offsets = ((jnp.arange(N_ITEM * SLOTS) // SLOTS) * COL_TILES).astype(jnp.int32)
    rows3 = vector.reshape(TILE_ROWS, TILE, K)

    def one_row(items):
        weight_row, rating_row, cols, block = items
        picked = table[(cols + offsets).astype(jnp.int32)].astype(jnp.float32)
        score = jnp.einsum("uk,sik->sui", block.astype(jnp.float32), picked)
        if with_ratings:
            mixed = (weight_row.astype(jnp.float32) * (rating_row.astype(jnp.float32) - score)).astype(jnp.bfloat16)
        else:
            mixed = (weight_row.astype(jnp.float32) * score).astype(jnp.bfloat16)
        return jnp.einsum("sui,sik->uk", mixed.astype(jnp.float32), picked)

    result = lax.map(one_row, (weights, ratings, tile_cols, rows3))
    return result.reshape(USERS, K)


def reference(weights, ratings, tile_cols, item_factors, old_users):
    table = item_factors.reshape(N_ITEM * COL_TILES, TILE, K)
    old_rounded = old_users.astype(jnp.bfloat16)
    residual = row_pass(table, weights, ratings, tile_cols, old_rounded, True) - ridge * old_users
    solution = old_users
    direction = residual
    norm_now = jnp.sum(residual * residual)
    for step in range(ITERS):
        rounded = direction.astype(jnp.bfloat16)
        image = row_pass(table, weights, ratings, tile_cols, rounded, False) + ridge * direction
        alpha = norm_now / jnp.sum(direction * image)
        solution = solution + alpha * direction
        residual = residual - alpha * image
        norm_next = jnp.sum(residual * residual)
        direction = residual + (norm_next / norm_now) * direction
        norm_now = norm_next
    blocks = solution.reshape(DEVS, DEVS, PIECE, K)
    return jnp.transpose(blocks, (1, 0, 2, 3)).reshape(USERS, K)
```

```python
import jax
import jax.numpy as jnp
from jax import lax
from jax.experimental import pallas as pl
from jax.experimental.pallas import tpu as pltpu
from jax.sharding import PartitionSpec as P

MESH = pl.DeviceIdType.MESH
BF = jnp.bfloat16
F32 = jnp.float32
RIDGE = 0.05
T = 128
SLOTS = 12
NI = 16
NU = 8
SH = 256


def near(a):
    return a + a // 2 - 2 * (a // 3)


def div(a, b):
    ok = b != 0.0
    return jnp.where(ok, a / jnp.where(ok, b, 1.0), 0.0)


def lanes(a):
    return jnp.sum(a, axis=0, keepdims=True)


def total(a):
    return jnp.broadcast_to(jnp.sum(a, axis=1, keepdims=True), (1, T))


def kernel(
    cols, w_hbm, r_hbm, i_hbm, x_hbm, out,
    w, rt, it, tt, x0, q0, q1, part, got, vec, wide, v0, y0, t1, y1, t2, acc, sj, og,
    us_in, us_out, ps_in, ps_out, xd_out, xd_in,
    w_sem, r_sem, i_sem, rs_s, rs_r, ag_s, ag_r, us_s, us_r, ps_s, ps_r, xd_s, xd_r,
):
    u = lax.axis_index("user")
    i = lax.axis_index("item")
    x, z = i // 4, lax.rem(i, 4)

    def shard(k):
        return lax.rem(x + near(k // 4), 4) * 4 + lax.rem(z + near(lax.rem(k, 4)), 4)

    def mate(k):
        return lax.rem(u + k, NU)

    bar = pltpu.get_barrier_semaphore()

    def greet_plane(k, c):
        pl.semaphore_signal(bar, inc=1, device_id=(u, shard(k)), device_id_type=MESH)
        return c

    def greet_user(k, c):
        pl.semaphore_signal(bar, inc=1, device_id=(mate(k), i), device_id_type=MESH)
        return c

    load_i = pltpu.make_async_copy(i_hbm, it, i_sem.at[0])
    load_x = pltpu.make_async_copy(x_hbm, x0, i_sem.at[1])

    def load_w(j):
        rows = pl.ds(2 * j, 2)
        return pltpu.make_async_copy(w_hbm.at[rows], w.at[rows], w_sem.at[j])

    def load_r(j):
        rows = pl.ds(2 * j, 2)
        return pltpu.make_async_copy(r_hbm.at[rows], rt.at[rows], r_sem.at[j])

    load_i.start()
    load_x.start()

    def start_loads(k, c):
        j = shard(15 - k)
        load_w(j).start()
        load_r(j).start()
        return c

    lax.fori_loop(0, NI, start_loads, 0)
    lax.fori_loop(1, NI, greet_plane, 0)
    lax.fori_loop(1, NU, greet_user, 0)

    load_i.wait()

    def turn(c, carry):
        tt[c] = it[c].T
        return carry

    lax.fori_loop(0, 32, turn, 0)
    load_x.wait()

    def rs_copy(n, j):
        return pltpu.make_async_remote_copy(
            src_ref=part.at[n, j], dst_ref=got.at[n, i], send_sem=rs_s.at[n, j], recv_sem=rs_r.at[n, i],
            device_id=(u, j), device_id_type=MESH)

    def rs_arrival(n, j):
        return pltpu.make_async_remote_copy(
            src_ref=part.at[n, j], dst_ref=got.at[n, j], send_sem=rs_s.at[n, j], recv_sem=rs_r.at[n, j],
            device_id=(u, j), device_id_type=MESH)

    def ag_copy(n, j):
        return pltpu.make_async_remote_copy(
            src_ref=vec.at[n, i], dst_ref=vec.at[n, i], send_sem=ag_s.at[n, j], recv_sem=ag_r.at[n, i],
            device_id=(u, j), device_id_type=MESH)

    def ag_arrival(n, j):
        return pltpu.make_async_remote_copy(
            src_ref=vec.at[n, i], dst_ref=vec.at[n, j], send_sem=ag_s.at[n, j], recv_sem=ag_r.at[n, j],
            device_id=(u, j), device_id_type=MESH)

    def us_copy(m, o, slot):
        return pltpu.make_async_remote_copy(
            src_ref=us_out.at[m], dst_ref=us_in.at[m, slot], send_sem=us_s.at[m, o], recv_sem=us_r.at[m, slot],
            device_id=(o, i), device_id_type=MESH)

    def ps_copy(m, j, slot):
        return pltpu.make_async_remote_copy(
            src_ref=ps_out.at[m], dst_ref=ps_in.at[m, slot], send_sem=ps_s.at[m, j], recv_sem=ps_r.at[m, slot],
            device_id=(u, j), device_id_type=MESH)

    def xd_copy(o, slot):
        return pltpu.make_async_remote_copy(
            src_ref=xd_out.at[pl.ds(pl.multiple_of(o * 64, 64), 64)], dst_ref=xd_in.at[slot],
            send_sem=xd_s.at[o], recv_sem=xd_r.at[slot], device_id=(o, i), device_id_type=MESH)

    def each(lo, hi, fn):
        def body(k, c):
            fn(k)
            return c
        lax.fori_loop(lo, hi, body, 0)

    def score_pair(d, r, p):
        t = jnp.concatenate([tt[cols[r, 2 * p]], tt[cols[r, 2 * p + 1]]], axis=1)
        return jnp.dot(d, t, preferred_element_type=F32)

    def weight_pair(ref, r, p):
        return jnp.concatenate([ref[r, 2 * p], ref[r, 2 * p + 1]], axis=1).astype(F32)

    def rows_of(n, j, h):
        if n == 0:
            return x0[pl.ds(pl.multiple_of(j * SH + h * T, T), T), :].astype(BF)
        d = vec[n - 1, j, h * T:(h + 1) * T, :]
        wide[n - 1, pl.ds(pl.multiple_of(j * SH + h * T, T), T), :] = d.astype(F32)
        return d

    def scores(n, j, q):
        for h in range(2):
            r = 2 * j + h
            d = rows_of(n, j, h)
            for p in range(SLOTS // 2):
                s = score_pair(d, r, p)
                if n == 0:
                    s = weight_pair(rt, r, p) - s
                q[h * T:(h + 1) * T, 2 * T * p:2 * T * (p + 1)] = (weight_pair(w, r, p) * s).astype(BF)

    def spread(n, j, q):
        for h in range(2):
            r = 2 * j + h
            items = jnp.concatenate([it[cols[r, b]] for b in range(SLOTS)], axis=0)
            part[n, j, h * T:(h + 1) * T, :] = jnp.dot(
                q[h * T:(h + 1) * T, :], items, preferred_element_type=F32).astype(BF)

    def run_pass(n):
        first = n == 0

        def at(k):
            return shard(15 - k) if first else shard(k)

        def ready(k):
            j = at(k)
            if first:
                load_w(j).wait()
                load_r(j).wait()
            else:
                ag_arrival(n - 1, j).wait_recv()

        if first:
            ready(0)
        scores(n, at(0), q0)

        def two(kk, c):
            a, b = at(2 * kk), at(2 * kk + 1)
            ready(2 * kk + 1)
            spread(n, a, q0)
            scores(n, b, q1)
            if first:
                @pl.when(kk == 0)
                def _():
                    pl.semaphore_wait(bar, NI - 1 + NU - 1)
                rs_copy(n, a).start()
            else:
                @pl.when(kk > 0)
                def _():
                    rs_copy(n, a).start()
            ready(2 * kk + 2)
            spread(n, b, q1)
            scores(n, at(2 * kk + 2), q0)
            rs_copy(n, b).start()
            return c

        lax.fori_loop(0, 7, two, 0)
        a, b = at(14), at(15)
        ready(15)
        spread(n, a, q0)
        scores(n, b, q1)
        rs_copy(n, a).start()
        spread(n, b, q1)
        if not first:
            rs_copy(n, b).start()

    def collect(n):
        acc[...] = part[n, i].astype(F32)

        def add(k):
            j = shard(k)
            rs_arrival(n, j).wait_recv()
            acc[...] += got[n, j].astype(F32)

        each(1, NI, add)
        return acc[...]

    def publish(n, value):
        vec[n, i] = value.astype(BF)
        each(1, NI, lambda k: ag_copy(n, shard(k)).start())

    def user_send(m):
        each(1, NU, lambda k: us_copy(m, mate(k), u).start())

    def user_sum(m):
        us_in[m, u] = us_out[m]

        def wait(k):
            us_copy(m, mate(k), mate(k)).wait_recv()

        each(1, NU, wait)
        return jnp.sum(us_in[m], axis=0)

    def plane_send(m):
        each(1, NI, lambda k: ps_copy(m, shard(k), i).start())

    def plane_sum(m):
        ps_in[m, i] = ps_out[m]

        def wait(k):
            ps_copy(m, shard(k), shard(k)).wait_recv()

        each(1, NI, wait)
        return jnp.sum(ps_in[m, :, 0:8, :], axis=0)

    def pick(tile, m):
        return total(tile[m:m + 1, :])

    zero = jnp.zeros((1, T), F32)
    mine = pl.ds(pl.multiple_of(i * SH, SH), SH)

    run_pass(0)
    v0[...] = collect(0) - RIDGE * x0[mine, :]
    publish(0, v0[...])
    vv = lanes(v0[...] * v0[...])

    run_pass(1)
    y0[...] = collect(1) + RIDGE * v0[...]
    vy = lanes(v0[...] * y0[...])
    inv_alpha = div(total(vy), total(vv))
    alpha = div(total(vv), total(vy))
    t1[...] = v0[...] - alpha * y0[...]
    publish(1, t1[...])
    us_out[0] = jnp.concatenate([vv, vy, zero, zero, zero, zero, zero, zero], axis=0)
    user_send(0)

    run_pass(2)
    ps_out[0, 0:8, :] = user_sum(0)
    ps_out[0, 8:16, :] = jnp.zeros((8, T), F32)
    plane_send(0)
    y1[...] = collect(2) + RIDGE * t1[...]
    tt1 = lanes(t1[...] * t1[...])
    beta_own = div(total(tt1), total(vv))
    vy1 = lanes(v0[...] * y1[...])
    ty0 = lanes(t1[...] * y0[...])
    ty1 = lanes(t1[...] * y1[...])
    dad_own = total(ty1 + beta_own * (ty0 + vy1) + beta_own * beta_own * vy)
    alpha1 = div(total(tt1), dad_own)
    inv_alpha1 = div(dad_own, total(tt1))
    t2[...] = t1[...] - alpha1 * (y1[...] + beta_own * y0[...])
    publish(2, t2[...])
    og[...] = jnp.concatenate([
        vy, ty0, ty1, lanes(t2[...] * y0[...]), lanes(t2[...] * y1[...]), lanes(t2[...] * t2[...]), zero, zero], axis=0)

    sums0 = plane_sum(0)
    rr0, vy_all = pick(sums0, 0), pick(sums0, 1)
    a0 = rr0 / vy_all
    rho = a0 * inv_alpha
    r1 = v0[...] - a0 * y0[...]
    z1 = rho * y1[...] + (1.0 - rho) * y0[...]
    us_out[1] = jnp.concatenate([
        lanes(r1 * r1), lanes(r1 * z1), lanes(r1 * y0[...]), lanes(v0[...] * z1), lanes(z1 * z1),
        lanes(z1 * y0[...]), lanes(y0[...] * y0[...]), zero], axis=0)
    user_send(1)
    ps_out[1, 8:16, :] = jnp.concatenate([inv_alpha, inv_alpha1, beta_own, zero, zero, zero, zero, zero], axis=0)

    def squares(k):
        j = shard(k)
        out_sum = jnp.zeros((8, T), F32)
        for h in range(2):
            r = 2 * j + h
            d = rows_of(3, j, h)
            part_sum = jnp.zeros((T, 2 * T), F32)
            for p in range(SLOTS // 2):
                s = score_pair(d, r, p)
                part_sum += weight_pair(w, r, p) * s * s
            out_sum += jnp.sum((part_sum[:, :T] + part_sum[:, T:]).reshape(T // 8, 8, T), axis=0)
        sj[j] = out_sum

    def arrive_squares(k):
        ag_arrival(2, shard(k)).wait_recv()
        squares(k)

    squares(0)
    each(1, 8, arrive_squares)
    ps_out[1, 0:8, :] = user_sum(1)
    plane_send(1)
    each(8, NI, arrive_squares)

    sums1 = plane_sum(1)
    rr1, r1z1, r1y0, v0z1, z1z1, z1y0, y0y0 = [pick(sums1, m) for m in range(7)]
    b0 = rr1 / rr0
    a1 = rr1 / (r1z1 + b0 * (r1y0 + v0z1) + b0 * b0 * vy_all)
    rr2 = rr1 - 2.0 * a1 * (r1z1 + b0 * r1y0) + a1 * a1 * (z1z1 + 2.0 * b0 * z1y0 + b0 * b0 * y0y0)
    b1 = rr2 / rr1

    def coefficients(inv_a, inv_a1, beta):
        rho = a0 * inv_a
        h = a1 * (rho * beta - 1.0 + rho - b0) * inv_a
        e0 = (1.0 - rho + h) + b1 * (1.0 - rho + b0)
        e1 = rho - a1 * rho * inv_a1 - h + b1 * rho
        e2 = a1 * rho * inv_a1
        return a0 + a1 * (1.0 - rho + b0), a1 * rho, e0, e1, e2

    _, _, e0, e1, e2 = coefficients(inv_alpha, inv_alpha1, beta_own)
    g = og[...]
    own = (e0 * e0 * g[0:1] + 2.0 * e0 * e1 * g[1:2] + e1 * e1 * g[2:3] + 2.0 * e0 * e2 * g[3:4]
           + 2.0 * e1 * e2 * g[4:5] + e2 * e2 * RIDGE * g[5:6])

    def weigh(p, tot):
        _, _, _, _, e2 = coefficients(ps_in[1, p, 8:9, :], ps_in[1, p, 9:10, :], ps_in[1, p, 10:11, :])
        return tot + e2 * e2 * lanes(sj[p])

    us_out[2] = jnp.concatenate([lax.fori_loop(0, NI, weigh, own), zero, zero, zero, zero, zero, zero, zero], axis=0)
    user_send(2)

    def choose(p):
        f0, f1, e0, e1, e2 = coefficients(ps_in[1, p, 8:9, :], ps_in[1, p, 9:10, :], ps_in[1, p, 10:11, :])
        for e in range(2):
            rows = pl.ds(p * SH + 2 * i + e, NU, stride=32)
            a, b, c = wide[0, rows, :], wide[1, rows, :], wide[2, rows, :]
            xd_out[pl.ds(2 * p + e, NU, stride=64), :] = x0[rows, :] + f0 * a + f1 * b
            xd_out[pl.ds(32 + 2 * p + e, NU, stride=64), :] = e0 * a + e1 * b + e2 * c

    each(0, NI, choose)
    each(1, NU, lambda k: xd_copy(mate(k), u).start())

    ps_out[2, 0:8, :] = user_sum(2)
    ps_out[2, 8:16, :] = jnp.zeros((8, T), F32)
    plane_send(2)
    xd_in[u] = xd_out[pl.ds(pl.multiple_of(u * 64, 64), 64), :]
    each(1, NU, lambda k: xd_copy(mate(k), mate(k)).wait_recv())
    a2 = rr2 / pick(plane_sum(2), 0)
    for o in range(NU):
        out[o * 32:(o + 1) * 32, :] = xd_in[o, 0:32, :] + a2 * xd_in[o, 32:64, :]

    def sent_plane(k):
        j = shard(k)
        for n in range(3):
            rs_copy(n, j).wait_send()
            ag_copy(n, j).wait_send()
            ps_copy(n, j, i).wait_send()

    def sent_user(k):
        o = mate(k)
        for m in range(3):
            us_copy(m, o, u).wait_send()
        xd_copy(o, u).wait_send()

    each(1, NI, sent_plane)
    each(1, NU, sent_user)


def shards(weights, ratings, tile_cols, item_factors, old_users):
    vmem = pltpu.VMEM
    dma = pltpu.SemaphoreType.DMA
    any_space = pl.BlockSpec(memory_space=pl.ANY)
    return pl.pallas_call(
        kernel,
        out_shape=jax.ShapeDtypeStruct((SH, T), F32),
        in_specs=[pl.BlockSpec(memory_space=pltpu.SMEM), any_space, any_space, any_space, any_space],
        out_specs=pl.BlockSpec(memory_space=vmem),
        scratch_shapes=[
            vmem((32, SLOTS, T, T), BF), vmem((32, SLOTS, T, T), BF),
            vmem((32, T, T), BF), vmem((32, T, T), BF), vmem((4096, T), F32),
            vmem((SH, SLOTS * T), BF), vmem((SH, SLOTS * T), BF),
            vmem((3, NI, SH, T), BF), vmem((3, NI, SH, T), BF), vmem((3, NI, SH, T), BF), vmem((3, 4096, T), F32),
            vmem((SH, T), F32), vmem((SH, T), F32), vmem((SH, T), F32), vmem((SH, T), F32), vmem((SH, T), F32), vmem((SH, T), F32),
            vmem((NI, 8, T), F32), vmem((8, T), F32),
            vmem((3, NU, 8, T), F32), vmem((3, 8, T), F32), vmem((3, NI, 16, T), F32), vmem((3, 16, T), F32),
            vmem((NU * 64, T), F32), vmem((NU, 64, T), F32),
            dma((NI,)), dma((NI,)), dma((2,)),
            dma((3, NI)), dma((3, NI)), dma((3, NI)), dma((3, NI)),
            dma((3, NU)), dma((3, NU)), dma((3, NI)), dma((3, NI)), dma((NU,)), dma((NU,)),
        ],
        compiler_params=pltpu.CompilerParams(
            collective_id=0, has_side_effects=True, vmem_limit_bytes=56 * 2 ** 20),
    )(tile_cols, weights, ratings, item_factors.reshape(32, T, T), old_users)


def solution(mesh):
    placed = (
        P("user", "item", None, None),
        P("user", "item", None, None),
        P("user", "item"),
        P("item", None),
        P("user", None),
    )
    return jax.shard_map(
        shards, mesh=mesh, in_specs=placed, out_specs=P(("user", "item"), None), check_vma=False
    )
```

```python
import jax
import jax.numpy as jnp
from jax import lax
from jax.experimental import pallas as pl
from jax.experimental.pallas import tpu as pltpu
from jax.sharding import PartitionSpec as P

MESH = pl.DeviceIdType.MESH
BF = jnp.bfloat16
F32 = jnp.float32
RIDGE = 0.05
T = 128
SLOTS = 12
NI = 16
NU = 8
SH = 256


def near(a):
    return a + a // 2 - 2 * (a // 3)


def div(a, b):
    ok = b != 0.0
    return jnp.where(ok, a / jnp.where(ok, b, 1.0), 0.0)


def lanes(a):
    return jnp.sum(a, axis=0, keepdims=True)


def total(a):
    return jnp.broadcast_to(jnp.sum(a, axis=1, keepdims=True), (1, T))


def kernel(
    c_hbm, w_hbm, r_hbm, i_hbm, x_hbm, out,
    w, rt, it, tt, x0, q0, q1, part, got, part2, got2, vec, wide, v0, y0, t1, y1, t2, sj, og,
    us_in, us_out, ps_in, ps_out, xd_out, xd_in, cols,
    w_sem, r_sem, i_sem, rs_s, rs_r, r2_s, r2_r, ag_s, ag_r, fw_s, fw_r, us_s, us_r, ps_s, ps_r, xd_s, xd_r,
):
    u = lax.axis_index("user")
    i = lax.axis_index("item")
    x, z = i // 4, lax.rem(i, 4)

    def at_offset(dx, dz):
        return lax.rem(x + dx, 4) * 4 + lax.rem(z + dz, 4)

    def shard(k):
        odd = lax.rem(k, 2)
        m = k - 7
        off = (k + 9) // 16
        dx = (1 - off) * odd * near((k + 1) // 2) + off * near(1 + m // 3)
        dz = (1 - off) * (1 - odd) * near(k // 2) + off * near(1 + lax.rem(m + 9, 3))
        return at_offset(dx, dz)

    def line_mate(axis, a):
        return at_offset(near(a), 0) if axis == 0 else at_offset(0, near(a))

    def mate(k):
        return lax.rem(u + k, NU)

    bar = pltpu.get_barrier_semaphore()

    def greet_plane(k, c):
        pl.semaphore_signal(bar, inc=1, device_id=(u, shard(k)), device_id_type=MESH)
        return c

    def greet_user(k, c):
        pl.semaphore_signal(bar, inc=1, device_id=(mate(k), i), device_id_type=MESH)
        return c

    load_i = pltpu.make_async_copy(i_hbm, it, i_sem.at[0])
    load_c = pltpu.make_async_copy(c_hbm, cols, i_sem.at[2])
    load_x = pltpu.make_async_copy(x_hbm, x0, i_sem.at[1])

    def load_w(j):
        rows = pl.ds(2 * j, 2)
        return pltpu.make_async_copy(w_hbm.at[rows], w.at[rows], w_sem.at[j])

    def load_r(j):
        rows = pl.ds(2 * j, 2)
        return pltpu.make_async_copy(r_hbm.at[rows], rt.at[rows], r_sem.at[j])

    load_c.start()
    load_i.start()
    load_x.start()

    def start_loads(k, c):
        j = shard(15 - k)
        load_w(j).start()
        load_r(j).start()
        return c

    lax.fori_loop(0, NI, start_loads, 0)
    lax.fori_loop(1, NI, greet_plane, 0)
    lax.fori_loop(1, NU, greet_user, 0)

    load_i.wait()

    def turn(c, carry):
        tt[c] = it[c].T
        return carry

    lax.fori_loop(0, 32, turn, 0)
    load_x.wait()
    load_c.wait()

    me = (x, z)

    def place(axis, line):
        return line * 4 + z if axis == 0 else x * 4 + line

    def rs_copy(n, h, j):
        jj = (j // 4, lax.rem(j, 4))
        return pltpu.make_async_remote_copy(
            src_ref=part.at[n, j, h * T:(h + 1) * T], dst_ref=got.at[n, h, me[1 - h], jj[h]], send_sem=rs_s.at[n, j, h],
            recv_sem=rs_r.at[n, h, me[1 - h], jj[h]], device_id=(u, place(1 - h, jj[1 - h])), device_id_type=MESH)

    def rs_arrival(n, h, line, group):
        return pltpu.make_async_remote_copy(
            src_ref=part.at[n, 0, 0:T], dst_ref=got.at[n, h, line, group], send_sem=rs_s.at[n, 0, h],
            recv_sem=rs_r.at[n, h, line, group], device_id=(u, place(1 - h, line)), device_id_type=MESH)

    def r2_copy(n, h, line, slot):
        return pltpu.make_async_remote_copy(
            src_ref=part2.at[n, h, line], dst_ref=got2.at[n, h, slot], send_sem=r2_s.at[n, h, line],
            recv_sem=r2_r.at[n, h, slot], device_id=(u, place(h, line)), device_id_type=MESH)

    def rs_send(n, j):
        @pl.when(lax.rem(j, 4) != z)
        def _():
            rs_copy(n, 0, j).start()

        @pl.when(j // 4 != x)
        def _():
            rs_copy(n, 1, j).start()

    def line_sum(n, h, group):
        total_ = part[n, place(h, group), h * T:(h + 1) * T, :].astype(F32)
        for a in range(1, 4):
            line = lax.rem(me[1 - h] + near(a), 4)
            rs_arrival(n, h, line, group).wait_recv()
            total_ += got[n, h, line, group].astype(F32)
        return total_

    def pass_on(n):
        for a in range(1, 4):
            for h in range(2):
                line = lax.rem(me[h] + near(a), 4)
                part2[n, h, line] = line_sum(n, h, line).astype(BF)
                r2_copy(n, h, line, me[h]).start()

    def ag_copy(n, j):
        return pltpu.make_async_remote_copy(
            src_ref=vec.at[n, i], dst_ref=vec.at[n, i], send_sem=ag_s.at[n, j], recv_sem=ag_r.at[n, i],
            device_id=(u, j), device_id_type=MESH)

    def ag_arrival(n, j):
        return pltpu.make_async_remote_copy(
            src_ref=vec.at[n, i], dst_ref=vec.at[n, j], send_sem=ag_s.at[n, j], recv_sem=ag_r.at[n, j],
            device_id=(u, j), device_id_type=MESH)

    def half(axis):
        return pl.ds(axis * T, T)

    def fw_copy(n, j, k, axis, a):
        rows = half(axis)
        return pltpu.make_async_remote_copy(
            src_ref=vec.at[n, j, rows], dst_ref=vec.at[n, j, rows], send_sem=fw_s.at[n, k, a - 1],
            recv_sem=fw_r.at[n, j, axis], device_id=(u, line_mate(1 - axis, a)), device_id_type=MESH)

    def line_in(n, k, axis):
        j = shard(k)
        ag_arrival(n, j).wait_recv()
        for a in range(1, 4):
            fw_copy(n, j, k, axis, a).start()

    def lines_in(n, m):
        line_in(n, 2 * m - 1, 0)
        line_in(n, 2 * m, 1)

    def vec_ready(n, k):
        @pl.when(k <= 3)
        def _():
            lines_in(n, k)

        @pl.when(k >= 7)
        def _():
            j = shard(k)
            for axis in range(2):
                fw_copy(n, j, 0, axis, 1).wait_recv()

    def us_copy(m, o, slot):
        return pltpu.make_async_remote_copy(
            src_ref=us_out.at[m], dst_ref=us_in.at[m, slot], send_sem=us_s.at[m, o], recv_sem=us_r.at[m, slot],
            device_id=(o, i), device_id_type=MESH)

    def ps_copy(m, j, slot):
        return pltpu.make_async_remote_copy(
            src_ref=ps_out.at[m], dst_ref=ps_in.at[m, slot], send_sem=ps_s.at[m, j], recv_sem=ps_r.at[m, slot],
            device_id=(u, j), device_id_type=MESH)

    def xd_copy(o, slot):
        return pltpu.make_async_remote_copy(
            src_ref=xd_out.at[pl.ds(pl.multiple_of(o * 64, 64), 64)], dst_ref=xd_in.at[slot],
            send_sem=xd_s.at[o], recv_sem=xd_r.at[slot], device_id=(o, i), device_id_type=MESH)

    def each(lo, hi, fn):
        def body(k, c):
            fn(k)
            return c
        lax.fori_loop(lo, hi, body, 0)

    def score_pair(d, r, p):
        t = jnp.concatenate([tt[cols[r, 2 * p]], tt[cols[r, 2 * p + 1]]], axis=1)
        return jnp.dot(d, t, preferred_element_type=F32)

    def weight_pair(ref, r, p):
        return jnp.concatenate([ref[r, 2 * p], ref[r, 2 * p + 1]], axis=1).astype(F32)

    def rows_of(n, j, h):
        if n == 0:
            return x0[pl.ds(pl.multiple_of(j * SH + h * T, T), T), :].astype(BF)
        d = vec[n - 1, j, h * T:(h + 1) * T, :]
        wide[n - 1, pl.ds(pl.multiple_of(j * SH + h * T, T), T), :] = d.astype(F32)
        return d

    def scores(n, j, q):
        for h in range(2):
            r = 2 * j + h
            d = rows_of(n, j, h)
            for p in range(SLOTS // 2):
                s = score_pair(d, r, p)
                if n == 0:
                    s = weight_pair(rt, r, p) - s
                q[h * T:(h + 1) * T, 2 * T * p:2 * T * (p + 1)] = (weight_pair(w, r, p) * s).astype(BF)

    def spread(n, j, q):
        for h in range(2):
            r = 2 * j + h
            items = jnp.concatenate([it[cols[r, b]] for b in range(SLOTS)], axis=0)
            part[n, j, h * T:(h + 1) * T, :] = jnp.dot(
                q[h * T:(h + 1) * T, :], items, preferred_element_type=F32).astype(BF)

    def run_pass(n):
        first = n == 0

        def at(k):
            return shard(15 - k) if first else shard(k)

        def ready(k):
            j = at(k)
            if first:
                load_w(j).wait()
                load_r(j).wait()
            else:
                vec_ready(n - 1, k)

        if first:
            ready(0)
        scores(n, at(0), q0)

        def two(kk, c):
            a, b = at(2 * kk), at(2 * kk + 1)
            ready(2 * kk + 1)
            spread(n, a, q0)
            scores(n, b, q1)
            if first:
                @pl.when(kk == 0)
                def _():
                    pl.semaphore_wait(bar, NI - 1 + NU - 1)
            rs_send(n, a)
            ready(2 * kk + 2)
            spread(n, b, q1)
            scores(n, at(2 * kk + 2), q0)
            rs_send(n, b)
            if n == 2:
                @pl.when(kk == 4)
                def _():
                    us_out[0] = plane_sum(0)
                    user_send(0)
            return c

        lax.fori_loop(0, 7, two, 0)
        a, b = at(14), at(15)
        ready(15)
        spread(n, a, q0)
        scores(n, b, q1)
        rs_send(n, a)
        if first:
            pass_on(n)
            spread(n, b, q1)
        else:
            spread(n, b, q1)
            rs_send(n, b)
            pass_on(n)

    def collect(n):
        halves = []
        for h in range(2):
            sum_ = line_sum(n, h, me[h])
            for a in range(1, 4):
                line = lax.rem(me[h] + near(a), 4)
                r2_copy(n, h, line, line).wait_recv()
                sum_ += got2[n, h, line].astype(F32)
            halves.append(sum_)
        return jnp.concatenate(halves, axis=0)

    def publish(n, value):
        vec[n, i] = value.astype(BF)
        each(1, 7, lambda k: ag_copy(n, shard(k)).start())

    def user_send(m):
        each(1, NU, lambda k: us_copy(m, mate(k), u).start())

    def user_sum(m):
        us_in[m, u] = us_out[m]

        def wait(k):
            us_copy(m, mate(k), mate(k)).wait_recv()

        each(1, NU, wait)
        return jnp.sum(us_in[m], axis=0)

    def plane_send(m):
        each(1, NI, lambda k: ps_copy(m, shard(k), i).start())

    def plane_sum(m):
        ps_in[m, i] = ps_out[m]

        def wait(k):
            ps_copy(m, shard(k), shard(k)).wait_recv()

        each(1, NI, wait)
        return jnp.sum(ps_in[m, :, 0:8, :], axis=0)

    def pick(tile, m):
        return total(tile[m:m + 1, :])

    zero = jnp.zeros((1, T), F32)
    mine = pl.ds(pl.multiple_of(i * SH, SH), SH)

    run_pass(0)
    v0[...] = collect(0) - RIDGE * x0[mine, :]
    publish(0, v0[...])
    vv = lanes(v0[...] * v0[...])

    run_pass(1)
    y0[...] = collect(1) + RIDGE * v0[...]
    vy = lanes(v0[...] * y0[...])
    inv_alpha = div(total(vy), total(vv))
    alpha = div(total(vv), total(vy))
    t1[...] = v0[...] - alpha * y0[...]
    publish(1, t1[...])
    ps_out[0, 0:8, :] = jnp.concatenate([vv, vy, zero, zero, zero, zero, zero, zero], axis=0)
    ps_out[0, 8:16, :] = jnp.zeros((8, T), F32)
    plane_send(0)

    run_pass(2)
    y1[...] = collect(2) + RIDGE * t1[...]
    tt1 = lanes(t1[...] * t1[...])
    beta_own = div(total(tt1), total(vv))
    vy1 = lanes(v0[...] * y1[...])
    ty0 = lanes(t1[...] * y0[...])
    ty1 = lanes(t1[...] * y1[...])
    dad_own = total(ty1 + beta_own * (ty0 + vy1) + beta_own * beta_own * vy)
    alpha1 = div(total(tt1), dad_own)
    inv_alpha1 = div(dad_own, total(tt1))
    t2[...] = t1[...] - alpha1 * (y1[...] + beta_own * y0[...])
    publish(2, t2[...])
    og[...] = jnp.concatenate([
        vy, ty0, ty1, lanes(t2[...] * y0[...]), lanes(t2[...] * y1[...]), lanes(t2[...] * t2[...]), zero, zero], axis=0)

    sums0 = user_sum(0)
    rr0, vy_all = pick(sums0, 0), pick(sums0, 1)
    a0 = rr0 / vy_all
    rho = a0 * inv_alpha
    r1 = v0[...] - a0 * y0[...]
    z1 = rho * y1[...] + (1.0 - rho) * y0[...]
    ps_out[1, 0:8, :] = jnp.concatenate([
        lanes(r1 * r1), lanes(r1 * z1), lanes(r1 * y0[...]), lanes(v0[...] * z1), lanes(z1 * z1),
        lanes(z1 * y0[...]), lanes(y0[...] * y0[...]), zero], axis=0)
    ps_out[1, 8:16, :] = jnp.concatenate([inv_alpha, inv_alpha1, beta_own, zero, zero, zero, zero, zero], axis=0)
    plane_send(1)

    def squares(k):
        j = shard(k)
        out_sum = jnp.zeros((8, T), F32)
        for h in range(2):
            r = 2 * j + h
            d = rows_of(3, j, h)
            part_sum = jnp.zeros((T, 2 * T), F32)
            for p in range(SLOTS // 2):
                s = score_pair(d, r, p)
                part_sum += weight_pair(w, r, p) * s * s
            out_sum += jnp.sum((part_sum[:, :T] + part_sum[:, T:]).reshape(T // 8, 8, T), axis=0)
        sj[j] = out_sum

    def arrive_squares(k):
        vec_ready(2, k)
        squares(k)

    squares(0)
    each(1, 10, arrive_squares)
    us_out[1] = plane_sum(1)
    user_send(1)
    each(10, NI, arrive_squares)

    sums1 = user_sum(1)
    rr1, r1z1, r1y0, v0z1, z1z1, z1y0, y0y0 = [pick(sums1, m) for m in range(7)]
    b0 = rr1 / rr0
    a1 = rr1 / (r1z1 + b0 * (r1y0 + v0z1) + b0 * b0 * vy_all)
    rr2 = rr1 - 2.0 * a1 * (r1z1 + b0 * r1y0) + a1 * a1 * (z1z1 + 2.0 * b0 * z1y0 + b0 * b0 * y0y0)
    b1 = rr2 / rr1

    def coefficients(inv_a, inv_a1, beta):
        rho = a0 * inv_a
        h = a1 * (rho * beta - 1.0 + rho - b0) * inv_a
        e0 = (1.0 - rho + h) + b1 * (1.0 - rho + b0)
        e1 = rho - a1 * rho * inv_a1 - h + b1 * rho
        e2 = a1 * rho * inv_a1
        return a0 + a1 * (1.0 - rho + b0), a1 * rho, e0, e1, e2

    _, _, e0, e1, e2 = coefficients(inv_alpha, inv_alpha1, beta_own)
    g = og[...]
    own = (e0 * e0 * g[0:1] + 2.0 * e0 * e1 * g[1:2] + e1 * e1 * g[2:3] + 2.0 * e0 * e2 * g[3:4]
           + 2.0 * e1 * e2 * g[4:5] + e2 * e2 * RIDGE * g[5:6])

    def weigh(p, tot):
        _, _, _, _, e2 = coefficients(ps_in[1, p, 8:9, :], ps_in[1, p, 9:10, :], ps_in[1, p, 10:11, :])
        return tot + e2 * e2 * lanes(sj[p])

    us_out[2] = jnp.concatenate([lax.fori_loop(0, NI, weigh, own), zero, zero, zero, zero, zero, zero, zero], axis=0)
    user_send(2)

    def choose(p):
        f0, f1, e0, e1, e2 = coefficients(ps_in[1, p, 8:9, :], ps_in[1, p, 9:10, :], ps_in[1, p, 10:11, :])
        for e in range(2):
            rows = pl.ds(p * SH + 2 * i + e, NU, stride=32)
            a, b, c = wide[0, rows, :], wide[1, rows, :], wide[2, rows, :]
            xd_out[pl.ds(2 * p + e, NU, stride=64), :] = x0[rows, :] + f0 * a + f1 * b
            xd_out[pl.ds(32 + 2 * p + e, NU, stride=64), :] = e0 * a + e1 * b + e2 * c

    each(0, NI, choose)
    each(1, NU, lambda k: xd_copy(mate(k), u).start())

    ps_out[2, 0:8, :] = user_sum(2)
    ps_out[2, 8:16, :] = jnp.zeros((8, T), F32)
    plane_send(2)
    xd_in[u] = xd_out[pl.ds(pl.multiple_of(u * 64, 64), 64), :]
    each(1, NU, lambda k: xd_copy(mate(k), mate(k)).wait_recv())
    a2 = rr2 / pick(plane_sum(2), 0)
    for o in range(NU):
        out[o * 32:(o + 1) * 32, :] = xd_in[o, 0:32, :] + a2 * xd_in[o, 32:64, :]

    def sent_plane(k):
        j = shard(k)
        for n in range(3):
            @pl.when(lax.rem(j, 4) != z)
            def _():
                rs_copy(n, 0, j).wait_send()

            @pl.when(j // 4 != x)
            def _():
                rs_copy(n, 1, j).wait_send()

            ps_copy(n, j, i).wait_send()

    def sent_lines(m):
        for n in range(3):
            for axis in range(2):
                k = 2 * m - 1 + axis
                j = shard(k)
                ag_copy(n, j).wait_send()
                r2_copy(n, axis, lax.rem(me[axis] + near(m), 4), me[axis]).wait_send()
                for a in range(1, 4):
                    fw_copy(n, j, k, axis, a).wait_send()

    def sent_user(k):
        o = mate(k)
        for m in range(3):
            us_copy(m, o, u).wait_send()
        xd_copy(o, u).wait_send()

    each(1, NI, sent_plane)
    each(1, 4, sent_lines)
    each(1, NU, sent_user)


def shards(weights, ratings, tile_cols, item_factors, old_users):
    vmem = pltpu.VMEM
    dma = pltpu.SemaphoreType.DMA
    any_space = pl.BlockSpec(memory_space=pl.ANY)
    return pl.pallas_call(
        kernel,
        out_shape=jax.ShapeDtypeStruct((SH, T), F32),
        in_specs=[any_space, any_space, any_space, any_space, any_space],
        out_specs=pl.BlockSpec(memory_space=vmem),
        scratch_shapes=[
            vmem((32, SLOTS, T, T), BF), vmem((32, SLOTS, T, T), BF),
            vmem((32, T, T), BF), vmem((32, T, T), BF), vmem((4096, T), F32),
            vmem((SH, SLOTS * T), BF), vmem((SH, SLOTS * T), BF),
            vmem((3, NI, SH, T), BF), vmem((3, 2, 4, 4, T, T), BF), vmem((3, 2, 4, T, T), BF), vmem((3, 2, 4, T, T), BF),
            vmem((3, NI, SH, T), BF), vmem((3, 4096, T), F32),
            vmem((SH, T), F32), vmem((SH, T), F32), vmem((SH, T), F32), vmem((SH, T), F32), vmem((SH, T), F32),
            vmem((NI, 8, T), F32), vmem((8, T), F32),
            vmem((3, NU, 8, T), F32), vmem((3, 8, T), F32), vmem((3, NI, 16, T), F32), vmem((3, 16, T), F32),
            vmem((NU * 64, T), F32), vmem((NU, 64, T), F32),
            pltpu.SMEM((32, SLOTS), jnp.int32),
            dma((NI,)), dma((NI,)), dma((3,)),
            dma((3, NI, 2)), dma((3, 2, 4, 4)), dma((3, 2, 4)), dma((3, 2, 4)), dma((3, NI)), dma((3, NI)), dma((3, 7, 3)), dma((3, NI, 2)),
            dma((3, NU)), dma((3, NU)), dma((3, NI)), dma((3, NI)), dma((NU,)), dma((NU,)),
        ],
        compiler_params=pltpu.CompilerParams(
            collective_id=0, has_side_effects=True, vmem_limit_bytes=56 * 2 ** 20),
    )(tile_cols, weights, ratings, item_factors.reshape(32, T, T), old_users)


def solution(mesh):
    placed = (
        P("user", "item", None, None),
        P("user", "item", None, None),
        P("user", "item"),
        P("item", None),
        P("user", None),
    )
    return jax.shard_map(
        shards, mesh=mesh, in_specs=placed, out_specs=P(("user", "item"), None), check_vma=False
    )
```

```python
import jax
import jax.numpy as jnp
from jax import lax
from jax.experimental import pallas as pl
from jax.experimental.pallas import tpu as pltpu
from jax.sharding import PartitionSpec as P

MESH = pl.DeviceIdType.MESH
BF = jnp.bfloat16
F32 = jnp.float32
RIDGE = 0.05
T = 128
SLOTS = 12
NI = 16
NU = 8
SH = 256


def quo(a, b):
    return a // b if isinstance(a, int) else lax.div(a, jnp.int32(b))


def near(a):
    return a + quo(a, 2) - 2 * quo(a + 1, 4)


def div(a, b):
    ok = b != 0.0
    return jnp.where(ok, a / jnp.where(ok, b, 1.0), 0.0)


def lanes(a):
    return jnp.sum(a, axis=0, keepdims=True)


def total(a):
    return jnp.broadcast_to(jnp.sum(a, axis=1, keepdims=True), (1, T))


def kernel(
    c_hbm, w_hbm, r_hbm, i_hbm, x_hbm, out,
    w, rt, it, x0, q0, q1, part, got, part2, got2, vec, wide, v0, y0, t1, y1, t2, sj, og,
    us_in, us_out, ps_in, ps_out, xd_out, xd_in, cols,
    w_sem, r_sem, i_sem, rs_s, rs_r, r2_s, r2_r, ag_s, ag_r, fw_s, fw_r, us_s, us_r, ps_s, ps_r, xd_s, xd_r,
):
    u = lax.axis_index("user")
    i = lax.axis_index("item")
    x, z = i // 4, lax.rem(i, 4)

    def at_offset(dx, dz):
        return lax.rem(x + dx, 4) * 4 + lax.rem(z + dz, 4)

    def shard(k):
        if isinstance(k, int):
            off, odd, m = k // 7 if k < 14 else 1, k % 2, max(k - 7, 0)
        else:
            off, odd, m = quo(k + 9, 16), lax.rem(k, 2), k - 7
        third = quo(m * 11, 32)
        dx = (1 - off) * odd * near(quo(k + 1, 2)) + off * near(1 + third)
        dz = (1 - off) * (1 - odd) * near(quo(k, 2)) + off * near(1 + m - 3 * third)
        return at_offset(dx, dz)

    def line_mate(axis, a):
        return at_offset(near(a), 0) if axis == 0 else at_offset(0, near(a))

    def mate(k):
        return lax.rem(u + k, NU)

    bar = pltpu.get_barrier_semaphore()

    def greet_plane(k, c):
        pl.semaphore_signal(bar, inc=1, device_id=(u, shard(k)), device_id_type=MESH)
        return c

    def greet_user(k, c):
        pl.semaphore_signal(bar, inc=1, device_id=(mate(k), i), device_id_type=MESH)
        return c

    load_i = pltpu.make_async_copy(i_hbm, it, i_sem.at[0])
    load_c = pltpu.make_async_copy(c_hbm, cols, i_sem.at[2])
    load_x = pltpu.make_async_copy(x_hbm, x0, i_sem.at[1])

    def load_w(j):
        rows = pl.ds(2 * j, 2)
        return pltpu.make_async_copy(w_hbm.at[rows], w.at[rows], w_sem.at[j])

    def load_r(j):
        rows = pl.ds(2 * j, 2)
        return pltpu.make_async_copy(r_hbm.at[rows], rt.at[rows], r_sem.at[j])

    load_c.start()
    load_i.start()
    load_x.start()

    def start_loads(k, c):
        j = shard(15 - k)
        load_w(j).start()
        load_r(j).start()
        return c

    lax.fori_loop(0, NI, start_loads, 0)
    lax.fori_loop(1, NI, greet_plane, 0)
    lax.fori_loop(1, NU, greet_user, 0)

    load_i.wait()

    load_x.wait()
    load_c.wait()

    me = (x, z)

    def place(axis, line):
        return line * 4 + z if axis == 0 else x * 4 + line

    def rs_copy(n, h, j):
        jj = (j // 4, lax.rem(j, 4))
        return pltpu.make_async_remote_copy(
            src_ref=part.at[n, j, h * T:(h + 1) * T], dst_ref=got.at[n, h, me[1 - h], jj[h]], send_sem=rs_s.at[n, j, h],
            recv_sem=rs_r.at[n, h, me[1 - h], jj[h]], device_id=(u, place(1 - h, jj[1 - h])), device_id_type=MESH)

    def rs_arrival(n, h, line, group):
        return pltpu.make_async_remote_copy(
            src_ref=part.at[n, 0, 0:T], dst_ref=got.at[n, h, line, group], send_sem=rs_s.at[n, 0, h],
            recv_sem=rs_r.at[n, h, line, group], device_id=(u, place(1 - h, line)), device_id_type=MESH)

    def r2_copy(n, h, line, slot):
        return pltpu.make_async_remote_copy(
            src_ref=part2.at[n, h, line], dst_ref=got2.at[n, h, slot], send_sem=r2_s.at[n, h, line],
            recv_sem=r2_r.at[n, h, slot], device_id=(u, place(h, line)), device_id_type=MESH)

    def rs_send(n, j):
        @pl.when(lax.rem(j, 4) != z)
        def _():
            rs_copy(n, 0, j).start()

        @pl.when(j // 4 != x)
        def _():
            rs_copy(n, 1, j).start()

    def line_sum(n, h, group):
        total_ = part[n, place(h, group), h * T:(h + 1) * T, :].astype(F32)
        for a in range(1, 4):
            line = lax.rem(me[1 - h] + near(a), 4)
            rs_arrival(n, h, line, group).wait_recv()
            total_ += got[n, h, line, group].astype(F32)
        return total_

    def pass_on(n):
        for a in range(1, 4):
            for h in range(2):
                line = lax.rem(me[h] + near(a), 4)
                part2[n, h, line] = line_sum(n, h, line).astype(BF)
                r2_copy(n, h, line, me[h]).start()

    def ag_copy(n, j):
        return pltpu.make_async_remote_copy(
            src_ref=vec.at[n, i], dst_ref=vec.at[n, i], send_sem=ag_s.at[n, j], recv_sem=ag_r.at[n, i],
            device_id=(u, j), device_id_type=MESH)

    def ag_arrival(n, j):
        return pltpu.make_async_remote_copy(
            src_ref=vec.at[n, i], dst_ref=vec.at[n, j], send_sem=ag_s.at[n, j], recv_sem=ag_r.at[n, j],
            device_id=(u, j), device_id_type=MESH)

    def half(axis):
        return pl.ds(axis * T, T)

    def fw_copy(n, j, k, axis, a):
        rows = half(axis)
        return pltpu.make_async_remote_copy(
            src_ref=vec.at[n, j, rows], dst_ref=vec.at[n, j, rows], send_sem=fw_s.at[n, k, a - 1],
            recv_sem=fw_r.at[n, j, axis], device_id=(u, line_mate(1 - axis, a)), device_id_type=MESH)

    def line_in(n, k, axis):
        j = shard(k)
        ag_arrival(n, j).wait_recv()
        for a in range(1, 4):
            fw_copy(n, j, k, axis, a).start()

    def lines_in(n, m):
        line_in(n, 2 * m - 1, 0)
        line_in(n, 2 * m, 1)

    def vec_ready(n, k):
        @pl.when(k <= 3)
        def _():
            lines_in(n, k)

        @pl.when(k >= 7)
        def _():
            j = shard(k)
            for axis in range(2):
                fw_copy(n, j, 0, axis, 1).wait_recv()

    def us_copy(m, o, slot):
        return pltpu.make_async_remote_copy(
            src_ref=us_out.at[m], dst_ref=us_in.at[m, slot], send_sem=us_s.at[m, o], recv_sem=us_r.at[m, slot],
            device_id=(o, i), device_id_type=MESH)

    def ps_copy(m, j, slot):
        return pltpu.make_async_remote_copy(
            src_ref=ps_out.at[m], dst_ref=ps_in.at[m, slot], send_sem=ps_s.at[m, j], recv_sem=ps_r.at[m, slot],
            device_id=(u, j), device_id_type=MESH)

    def xd_copy(o, slot):
        return pltpu.make_async_remote_copy(
            src_ref=xd_out.at[pl.ds(pl.multiple_of(o * 64, 64), 64)], dst_ref=xd_in.at[slot],
            send_sem=xd_s.at[o], recv_sem=xd_r.at[slot], device_id=(o, i), device_id_type=MESH)

    def each(lo, hi, fn):
        def body(k, c):
            fn(k)
            return c
        lax.fori_loop(lo, hi, body, 0)

    def score_pair(d, r, p):
        t = jnp.concatenate([it[cols[2 * p, r]], it[cols[2 * p + 1, r]]], axis=0)
        return lax.dot_general(d, t, (((1,), (1,)), ((), ())), preferred_element_type=F32)

    def weight_pair(ref, r, p):
        return jnp.concatenate([ref[r, 2 * p], ref[r, 2 * p + 1]], axis=1).astype(F32)

    def rows_of(n, j, h):
        if n == 0:
            return x0[pl.ds(pl.multiple_of(j * SH + h * T, T), T), :].astype(BF)
        d = vec[n - 1, j, h * T:(h + 1) * T, :]
        wide[n - 1, pl.ds(pl.multiple_of(j * SH + h * T, T), T), :] = d.astype(F32)
        return d

    def scores(n, j, q):
        for h in range(2):
            r = 2 * j + h
            d = rows_of(n, j, h)
            for p in range(SLOTS // 2):
                s = score_pair(d, r, p)
                if n == 0:
                    s = weight_pair(rt, r, p) - s
                q[h * T:(h + 1) * T, 2 * T * p:2 * T * (p + 1)] = (weight_pair(w, r, p) * s).astype(BF)

    def spread(n, j, q):
        for h in range(2):
            r = 2 * j + h
            items = jnp.concatenate([it[cols[b, r]] for b in range(SLOTS)], axis=0)
            part[n, j, h * T:(h + 1) * T, :] = jnp.dot(
                q[h * T:(h + 1) * T, :], items, preferred_element_type=F32).astype(BF)

    def run_pass(n):
        first = n == 0

        def at(k):
            return shard(15 - k) if first else shard(k)

        def ready(k):
            j = at(k)
            if first:
                load_w(j).wait()
                load_r(j).wait()
            else:
                vec_ready(n - 1, k)

        if first:
            ready(0)
        scores(n, at(0), q0)

        def two(kk, c):
            a, b = at(2 * kk), at(2 * kk + 1)
            ready(2 * kk + 1)
            spread(n, a, q0)
            scores(n, b, q1)
            if first:
                @pl.when(kk == 2)
                def _():
                    pl.semaphore_wait(bar, NI - 1 + NU - 1)
                    for k in range(4):
                        rs_send(n, at(k))

                @pl.when(kk >= 2)
                def _():
                    rs_send(n, a)
            else:
                rs_send(n, a)
            ready(2 * kk + 2)
            spread(n, b, q1)
            scores(n, at(2 * kk + 2), q0)
            if first:
                @pl.when(kk >= 2)
                def _():
                    rs_send(n, b)
            else:
                rs_send(n, b)
            if n == 2:
                @pl.when(kk == 4)
                def _():
                    us_out[0] = plane_sum(0)
                    user_send(0)
            return c

        lax.fori_loop(0, 7, two, 0)
        a, b = at(14), at(15)
        ready(15)
        spread(n, a, q0)
        scores(n, b, q1)
        rs_send(n, a)
        if first:
            pass_on(n)
            spread(n, b, q1)
        else:
            spread(n, b, q1)
            rs_send(n, b)
            pass_on(n)

    def collect(n):
        halves = []
        for h in range(2):
            sum_ = line_sum(n, h, me[h])
            for a in range(1, 4):
                line = lax.rem(me[h] + near(a), 4)
                r2_copy(n, h, line, line).wait_recv()
                sum_ += got2[n, h, line].astype(F32)
            halves.append(sum_)
        return jnp.concatenate(halves, axis=0)

    def publish(n, value):
        vec[n, i] = value.astype(BF)
        each(1, 7, lambda k: ag_copy(n, shard(k)).start())

    def user_send(m):
        each(1, NU, lambda k: us_copy(m, mate(k), u).start())

    def user_sum(m):
        us_in[m, u] = us_out[m]

        def wait(k):
            us_copy(m, mate(k), mate(k)).wait_recv()

        each(1, NU, wait)
        return jnp.sum(us_in[m], axis=0)

    def plane_send(m):
        each(1, NI, lambda k: ps_copy(m, shard(k), i).start())

    def plane_sum(m):
        ps_in[m, i] = ps_out[m]

        def wait(k):
            ps_copy(m, shard(k), shard(k)).wait_recv()

        each(1, NI, wait)
        return jnp.sum(ps_in[m, :, 0:8, :], axis=0)

    def pick(tile, m):
        return total(tile[m:m + 1, :])

    zero = jnp.zeros((1, T), F32)
    mine = pl.ds(pl.multiple_of(i * SH, SH), SH)

    run_pass(0)
    v0[...] = collect(0) - RIDGE * x0[mine, :]
    publish(0, v0[...])
    vv = lanes(v0[...] * v0[...])

    run_pass(1)
    y0[...] = collect(1) + RIDGE * v0[...]
    vy = lanes(v0[...] * y0[...])
    inv_alpha = div(total(vy), total(vv))
    alpha = div(total(vv), total(vy))
    t1[...] = v0[...] - alpha * y0[...]
    publish(1, t1[...])
    ps_out[0, 0:8, :] = jnp.concatenate([vv, vy, zero, zero, zero, zero, zero, zero], axis=0)
    ps_out[0, 8:16, :] = jnp.zeros((8, T), F32)
    plane_send(0)

    run_pass(2)
    y1[...] = collect(2) + RIDGE * t1[...]
    tt1 = lanes(t1[...] * t1[...])
    beta_own = div(total(tt1), total(vv))
    vy1 = lanes(v0[...] * y1[...])
    ty0 = lanes(t1[...] * y0[...])
    ty1 = lanes(t1[...] * y1[...])
    dad_own = total(ty1 + beta_own * (ty0 + vy1) + beta_own * beta_own * vy)
    alpha1 = div(total(tt1), dad_own)
    inv_alpha1 = div(dad_own, total(tt1))
    t2[...] = t1[...] - alpha1 * (y1[...] + beta_own * y0[...])
    publish(2, t2[...])
    og[...] = jnp.concatenate([
        vy, ty0, ty1, lanes(t2[...] * y0[...]), lanes(t2[...] * y1[...]), lanes(t2[...] * t2[...]), zero, zero], axis=0)

    sums0 = user_sum(0)
    rr0, vy_all = pick(sums0, 0), pick(sums0, 1)
    a0 = rr0 / vy_all
    rho = a0 * inv_alpha
    r1 = v0[...] - a0 * y0[...]
    z1 = rho * y1[...] + (1.0 - rho) * y0[...]
    ps_out[1, 0:8, :] = jnp.concatenate([
        lanes(r1 * r1), lanes(r1 * z1), lanes(r1 * y0[...]), lanes(v0[...] * z1), lanes(z1 * z1),
        lanes(z1 * y0[...]), lanes(y0[...] * y0[...]), zero], axis=0)
    ps_out[1, 8:16, :] = jnp.concatenate([inv_alpha, inv_alpha1, beta_own, zero, zero, zero, zero, zero], axis=0)
    plane_send(1)

    def squares(k):
        j = shard(k)
        out_sum = jnp.zeros((8, T), F32)
        for h in range(2):
            r = 2 * j + h
            d = rows_of(3, j, h)
            part_sum = jnp.zeros((T, 2 * T), F32)
            for p in range(SLOTS // 2):
                s = score_pair(d, r, p)
                part_sum += weight_pair(w, r, p) * s * s
            out_sum += jnp.sum((part_sum[:, :T] + part_sum[:, T:]).reshape(T // 8, 8, T), axis=0)
        sj[j] = out_sum

    def arrive_squares(k):
        vec_ready(2, k)
        squares(k)

    squares(0)
    each(1, 5, arrive_squares)
    us_out[1] = plane_sum(1)
    user_send(1)
    each(5, NI, arrive_squares)

    sums1 = user_sum(1)
    rr1, r1z1, r1y0, v0z1, z1z1, z1y0, y0y0 = [pick(sums1, m) for m in range(7)]
    b0 = rr1 / rr0
    a1 = rr1 / (r1z1 + b0 * (r1y0 + v0z1) + b0 * b0 * vy_all)
    rr2 = rr1 - 2.0 * a1 * (r1z1 + b0 * r1y0) + a1 * a1 * (z1z1 + 2.0 * b0 * z1y0 + b0 * b0 * y0y0)
    b1 = rr2 / rr1

    def coefficients(inv_a, inv_a1, beta):
        rho = a0 * inv_a
        h = a1 * (rho * beta - 1.0 + rho - b0) * inv_a
        e0 = (1.0 - rho + h) + b1 * (1.0 - rho + b0)
        e1 = rho - a1 * rho * inv_a1 - h + b1 * rho
        e2 = a1 * rho * inv_a1
        return a0 + a1 * (1.0 - rho + b0), a1 * rho, e0, e1, e2

    _, _, e0, e1, e2 = coefficients(inv_alpha, inv_alpha1, beta_own)
    g = og[...]
    own = (e0 * e0 * g[0:1] + 2.0 * e0 * e1 * g[1:2] + e1 * e1 * g[2:3] + 2.0 * e0 * e2 * g[3:4]
           + 2.0 * e1 * e2 * g[4:5] + e2 * e2 * RIDGE * g[5:6])

    def weigh(p, tot):
        _, _, _, _, e2 = coefficients(ps_in[1, p, 8:9, :], ps_in[1, p, 9:10, :], ps_in[1, p, 10:11, :])
        return tot + e2 * e2 * lanes(sj[p])

    us_out[2] = jnp.concatenate([lax.fori_loop(0, NI, weigh, own), zero, zero, zero, zero, zero, zero, zero], axis=0)
    user_send(2)

    def choose(p):
        f0, f1, e0, e1, e2 = coefficients(ps_in[1, p, 8:9, :], ps_in[1, p, 9:10, :], ps_in[1, p, 10:11, :])
        for e in range(2):
            rows = pl.ds(p * SH + 2 * i + e, NU, stride=32)
            a, b, c = wide[0, rows, :], wide[1, rows, :], wide[2, rows, :]
            xd_out[pl.ds(2 * p + e, NU, stride=64), :] = x0[rows, :] + f0 * a + f1 * b
            xd_out[pl.ds(32 + 2 * p + e, NU, stride=64), :] = e0 * a + e1 * b + e2 * c

    each(0, NI, choose)
    each(1, NU, lambda k: xd_copy(mate(k), u).start())

    ps_out[2, 0:8, :] = user_sum(2)
    ps_out[2, 8:16, :] = jnp.zeros((8, T), F32)
    plane_send(2)
    xd_in[u] = xd_out[pl.ds(pl.multiple_of(u * 64, 64), 64), :]
    each(1, NU, lambda k: xd_copy(mate(k), mate(k)).wait_recv())
    def sent_plane(k):
        j = shard(k)
        for n in range(3):
            @pl.when(lax.rem(j, 4) != z)
            def _():
                rs_copy(n, 0, j).wait_send()

            @pl.when(j // 4 != x)
            def _():
                rs_copy(n, 1, j).wait_send()

            if n < 2:
                ps_copy(n, j, i).wait_send()

    def sent_lines(m):
        for n in range(3):
            for axis in range(2):
                k = 2 * m - 1 + axis
                j = shard(k)
                ag_copy(n, j).wait_send()
                r2_copy(n, axis, lax.rem(me[axis] + near(m), 4), me[axis]).wait_send()
                for a in range(1, 4):
                    fw_copy(n, j, k, axis, a).wait_send()

    def sent_user(k):
        o = mate(k)
        for m in range(3):
            us_copy(m, o, u).wait_send()
        xd_copy(o, u).wait_send()

    each(1, NI, sent_plane)
    each(1, 4, sent_lines)
    each(1, NU, sent_user)

    a2 = rr2 / pick(plane_sum(2), 0)
    for o in range(NU):
        out[o * 32:(o + 1) * 32, :] = xd_in[o, 0:32, :] + a2 * xd_in[o, 32:64, :]
    each(1, NI, lambda k: ps_copy(2, shard(k), i).wait_send())


def shards(weights, ratings, tile_cols, item_factors, old_users):
    vmem = pltpu.VMEM
    dma = pltpu.SemaphoreType.DMA
    any_space = pl.BlockSpec(memory_space=pl.ANY)
    return pl.pallas_call(
        kernel,
        out_shape=jax.ShapeDtypeStruct((SH, T), F32),
        in_specs=[any_space, any_space, any_space, any_space, any_space],
        out_specs=pl.BlockSpec(memory_space=vmem),
        scratch_shapes=[
            vmem((32, SLOTS, T, T), BF), vmem((32, SLOTS, T, T), BF),
            vmem((32, T, T), BF), vmem((4096, T), F32),
            vmem((SH, SLOTS * T), BF), vmem((SH, SLOTS * T), BF),
            vmem((3, NI, SH, T), BF), vmem((3, 2, 4, 4, T, T), BF), vmem((3, 2, 4, T, T), BF), vmem((3, 2, 4, T, T), BF),
            vmem((3, NI, SH, T), BF), vmem((3, 4096, T), F32),
            vmem((SH, T), F32), vmem((SH, T), F32), vmem((SH, T), F32), vmem((SH, T), F32), vmem((SH, T), F32),
            vmem((NI, 8, T), F32), vmem((8, T), F32),
            vmem((3, NU, 8, T), F32), vmem((3, 8, T), F32), vmem((3, NI, 16, T), F32), vmem((3, 16, T), F32),
            vmem((NU * 64, T), F32), vmem((NU, 64, T), F32),
            pltpu.SMEM((SLOTS, 32), jnp.int32),
            dma((NI,)), dma((NI,)), dma((3,)),
            dma((3, NI, 2)), dma((3, 2, 4, 4)), dma((3, 2, 4)), dma((3, 2, 4)), dma((3, NI)), dma((3, NI)), dma((3, 7, 3)), dma((3, NI, 2)),
            dma((3, NU)), dma((3, NU)), dma((3, NI)), dma((3, NI)), dma((NU,)), dma((NU,)),
        ],
        compiler_params=pltpu.CompilerParams(
            collective_id=0, has_side_effects=True, vmem_limit_bytes=56 * 2 ** 20),
    )(tile_cols.T, weights, ratings, item_factors.reshape(32, T, T), old_users)


def solution(mesh):
    placed = (
        P("user", "item", None, None),
        P("user", "item", None, None),
        P("user", "item"),
        P("item", None),
        P("user", None),
    )
    return jax.shard_map(
        shards, mesh=mesh, in_specs=placed, out_specs=P(("user", "item"), None), check_vma=False
    )
```
